32 devices in a mesh: sweep: 2 (over y), rows: 8 (over z, x), coef: 2 (over core).
Axes of the slice: x: 2, y: 2, z: 4, core: 2. Of those that a mesh axis runs over, the one named last changes fastest.
Arguments:
- snapshots: bfloat16 [8192, 128], P(('sweep', 'rows')), parts along dimension 0, may hold values from -34 to 34
- panel_order: int32 [8192], P(('sweep', 'rows')), parts along dimension 0, may hold values from 0 to 511, as said below
- tile_values: bfloat16 [16, 16, 4, 256, 256], P(('sweep', 'coef'), 'rows'), parts along dimension 0, may hold values from -0.1875 to 0.1875
- self_coef: float32 [16, 4096], P(('sweep', 'coef'), 'rows'), parts along dimension 0, may hold values from 0.5 to 4
- col_index: int32 [16, 16, 4], P(('sweep', 'coef'), 'rows'), parts along dimension 0, may hold values from 0 to 15, as said below
- frequency: float32 [2], P('sweep'), parts along dimension 0, may hold values from -0.95 to 0.95
Outputs:
- sampled_image: bfloat16 [8192, 128], P(('sweep', 'rows'), 'coef'), parts along dimension 0
- projected: float32 [16, 128, 128], P(('sweep', 'coef')), parts along dimension 0
The draws below stay inside these ranges and needn't reach their ends.
There are 2 independent parts, one for each index of `sweep`. The reference program is written for one: setup_inputs(seed, part) draws one part's arguments, and reference() takes and returns one part's arrays. A program takes and returns all parts, laid end to end along the dimension named above; each array names one. Nothing has to cross between parts.
Inputs may be any that keep to these rules, and one draw needn't show every extreme that they name: `panel_order`: each aligned block of 512 entries starting at a multiple of 512 is a permutation of 0 to 511. `col_index`: entry [k, b, n] is the column block of tile n of block row b of operator k; entry n = 0 is b itself, entry n = 1 lies exactly 2 blocks from b, and every entry lies within 2 blocks of b.
All inputs are finite; a program needn't handle non-finite values.
Results may differ from the reference program's by a relative error of at most 0.0095.
Values may be sent and summed in bfloat16 or wider, within the bound.
A program may use at most 64 MiB of HBM per device.

```python
import math
import jax
import jax.numpy as jnp
from jax import lax

R = 128
TILE = 256
K = 8
NNZ = 4
BLK_DEV = 2
NB = 16
SLAB = 512
NP = 4096
N_ROWS = 8


def draw_snapshots(key, part):
    key_noise, key_common, key_rows, key_cols = jax.random.split(key, 4)
    noise = jnp.clip(jax.random.normal(key_noise, (NP, R), jnp.float32), -4.0, 4.0)
    common = 0.7 * jnp.clip(jax.random.normal(key_common, (NP, 1), jnp.float32), -4.0, 4.0)
    row_scale = jnp.exp(jax.random.uniform(key_rows, (NP, 1), jnp.float32, 0.0, math.log(10.0)))
    col_scale = jnp.exp(jax.random.uniform(key_cols, (1, R), jnp.float32, 0.0, math.log(10.0)))
    slab_index = (jnp.arange(NP) // SLAB).astype(jnp.float32)
    rising = 1.0 + 2.0 * slab_index / max(NB // BLK_DEV - 1, 1)
    return (0.015 * (noise + common) * row_scale * col_scale * rising[:, None]).astype(jnp.bfloat16)


def draw_panel_order(key, part):
    slab_count = NP // SLAB
    scores = jax.random.randint(key, (slab_count, SLAB), 0, 1 << 16) * SLAB + jnp.arange(SLAB)[None, :]
    return jnp.argsort(scores, axis=1, stable=True).reshape(NP).astype(jnp.int32)


def draw_col_index(key, part):
    key_offsets, key_sides = jax.random.split(key, 2)
    row_block = jnp.broadcast_to(jnp.arange(NB, dtype=jnp.int32)[None, :, None], (K, NB, 1))
    offsets = jax.random.randint(key_offsets, (K, NB, NNZ), -BLK_DEV, BLK_DEV + 1)
    side_sign = jax.random.randint(key_sides, (K, NB, 1), 0, 2) * 2 - 1
    far_block = row_block + side_sign * BLK_DEV
    far_block = jnp.where(far_block < 0, row_block + BLK_DEV, far_block)
    far_block = jnp.where(far_block >= NB, row_block - BLK_DEV, far_block)
    near_block = jnp.clip(row_block + offsets, 0, NB - 1)
    return jnp.concatenate([row_block, far_block, near_block[:, :, 2:]], axis=2).astype(jnp.int32)


def levels(own_key, dims, pieces, smallest, high):
    loudness, own = 1.0, jax.random.fold_in(own_key, 6)
    for axis_at, shards_of in pieces:
        draws = jnp.exp(jax.random.uniform(jax.random.fold_in(own, axis_at), (shards_of,), jnp.float32, smallest / len(pieces), high / len(pieces)))
        loudness = loudness * jnp.repeat(draws, dims[axis_at] // shards_of).reshape([-1 if axis == axis_at else 1 for axis in range(len(dims))])
    return loudness


def scatter_about(key, dims, deviation, reach, pieces=(), held_as=jnp.bfloat16):
    gain = levels(key, dims, pieces, -0.22, 0.18) if pieces else 1.0
    drawn = jax.random.normal(key, dims, jnp.float32) * deviation * gain
    return jnp.minimum(jnp.maximum(drawn, -reach), reach).astype(held_as)


def setup_inputs(seed: int = 0, part: int = 0) -> dict:
    seeds = jax.random.split(jax.random.key(seed), 7)
    part_splits = jax.random.split(jax.random.fold_in(seeds[6], part), 7)
    return {
        "snapshots": draw_snapshots(jax.random.fold_in(jax.random.fold_in(seeds[6], part), 71), part),
        "panel_order": draw_panel_order(jax.random.fold_in(jax.random.fold_in(seeds[6], part), 71), part),
        "tile_values": scatter_about(part_splits[2], (K, NB, NNZ, TILE, TILE), (NNZ * TILE) ** -0.5, 0.1875, ((0, 2), (1, 8))),
        "self_coef": jnp.clip(jnp.exp(math.log(4.0) - 2.0794415 * jax.random.uniform(part_splits[3], (K, NP), jnp.float32) ** levels(part_splits[3], (K, NP), ((0, 2), (1, 8)), -0.2, 0.2)), 0.5, 4.0),
        "col_index": draw_col_index(jax.random.fold_in(jax.random.fold_in(seeds[6], part), 71), part),
        "frequency": jnp.clip(jax.random.uniform(part_splits[5], (1,), jnp.float32, -0.95, 0.95), -0.95, 0.95),
    }


def chebyshev(point):
    values_list = [jnp.ones_like(point), point]
    for degree in range(2, K):
        values_list.append(2.0 * point * values_list[-1] - values_list[-2])
    return jnp.stack(values_list[:K])

def sandwich(factor, matrix):
    inner = jax.scipy.linalg.solve_triangular(factor, matrix, lower=True)
    return jax.scipy.linalg.solve_triangular(factor, inner.T, lower=True).T

def reorder_slab(slab_rows, positions):
    return slab_rows[positions]

def reference(snapshots, panel_order, tile_values, self_coef, col_index, frequency):
    geometric = snapshots.reshape(N_ROWS, SLAB, R)
    local_order = panel_order.reshape(N_ROWS, SLAB).astype(jnp.int32)
    ordered = jax.vmap(reorder_slab)(geometric, local_order).reshape(NP, R)
    ordered_wide = ordered.astype(jnp.float32)
    blocks_wide = ordered_wide.reshape(NB, TILE, R)
    weights = chebyshev(frequency[0])

    def one_operator(carry, inputs):
        tile_block, column_blocks, self_terms, weight_now = inputs
        picked = blocks_wide[column_blocks]
        near_field = jnp.einsum('bnij,bnjr->bir', tile_block.astype(jnp.float32), picked, precision=lax.Precision.HIGHEST)
        image = (near_field.reshape(NP, R) + self_terms[:, None] * ordered_wide).astype(jnp.bfloat16)
        image_wide = image.astype(jnp.float32)
        projection = jnp.dot(ordered_wide.T, image_wide, precision=lax.Precision.HIGHEST)
        return (carry + weight_now * image_wide, projection)
    total, projection = lax.scan(one_operator, jnp.zeros((NP, R), jnp.float32), (tile_values, col_index, self_coef, weights))
    gram = jnp.dot(ordered.T.astype(jnp.float32), ordered.astype(jnp.float32), preferred_element_type=jnp.float32)
    factor = jnp.linalg.cholesky(gram)
    projected = jax.vmap(sandwich, in_axes=(None, 0))(factor, projection)
    return (total.astype(jnp.bfloat16), projected)
```

```python
import functools

import jax
import jax.numpy as jnp
from jax import lax
from jax.experimental import pallas as pl
from jax.experimental.pallas import tpu as pltpu
from jax.sharding import PartitionSpec as P

K = 8
MESH = pl.DeviceIdType.MESH
HIGHEST = lax.Precision.HIGHEST
F32 = jnp.float32


def chebyshev(point):
    values = [jnp.float32(1.0), point]
    for _ in range(2, K):
        values.append(2.0 * point * values[-1] - values[-2])
    return values


def inverse_factor(a, w_ref):
    n = a.shape[0]
    row = lax.broadcasted_iota(jnp.int32, (n, n), 0)
    column = lax.broadcasted_iota(jnp.int32, (n, n), 1)
    right = jnp.where(row == column, 1.0, 0.0).astype(F32)
    rows8 = lax.broadcasted_iota(jnp.int32, (8, n), 0)
    for r0 in range(0, n, 8):
        rest = n - r0 - 8
        sa, sr, ta, tr = a[:8], right[:8], a[8:], right[8:]
        sc = [jnp.broadcast_to(sa[:, r0 + j : r0 + j + 1], (8, n)) for j in range(8)]
        if rest:
            tc = [jnp.broadcast_to(ta[:, r0 + j : r0 + j + 1], (rest, n)) for j in range(8)]
        scale = jnp.zeros((8, n), F32)
        for j in range(8):
            pivot = jnp.broadcast_to(sc[j][j : j + 1], (8, n))
            inverse = 1.0 / pivot
            factors = jnp.where(rows8 > j, sc[j] * inverse, 0.0)
            y = lax.rsqrt(pivot)
            y = y * (1.5 - 0.5 * pivot * y * y)
            scale = jnp.where(rows8 == j, y, scale)
            row_a, row_r = sa[j : j + 1], sr[j : j + 1]
            heads = [sc[i][j : j + 1] for i in range(8)]
            for i in range(j + 1, 8):
                sc[i] = sc[i] - factors * heads[i]
            sa = sa - factors * row_a
            sr = sr - factors * row_r
            if rest:
                below = tc[j] * inverse[:1]
                for i in range(j + 1, 8):
                    tc[i] = tc[i] - below * heads[i]
                ta = ta - below * row_a
                tr = tr - below * row_r
        w_ref[r0 : r0 + 8, :] = sr * scale
        a, right = ta, tr


def kernel(
    n, snap_ref, order_ref, tiles_ref, coef_ref, col_ref, freq_ref,
    sampled_ref, projected_ref,
    tiles, panels, acc, gsend, grecv, gsum, gall, w, wt, psend, precv, tsend, tall, wsend, wrecv,
    tile_sem, gs_sem, gr_sem, as_sem, ar_sem, hs_sem, hr_sem, fs_sem, fr_sem,
    ps_sem, pr_sem, ts_sem, tr_sem, ws_sem, wr_sem,
):
    me = lax.axis_index("rows")
    half = lax.axis_index("coef")
    other = 1 - half
    ops, blocks, per_row, tile_rows = tiles.shape[:4]
    slab, rank = snap_ref.shape
    per_op = n // ops
    t_rows = rank // per_op

    def peers(step):
        if n <= 8:
            for d in range(1, n):
                step(d, lax.rem(me + d, n))
        else:
            @pl.loop(1, n)
            def _(d):
                step(d, lax.rem(me + d, n))

    load = [
        pltpu.make_async_copy(tiles_ref.at[k], tiles.at[k], tile_sem.at[k]) for k in range(ops)
    ]
    for copy in load:
        copy.start()

    barrier = pltpu.get_barrier_semaphore()
    peers(lambda d, peer: pl.semaphore_signal(
        barrier, inc=1, device_id={"rows": peer}, device_id_type=MESH))
    pl.semaphore_signal(barrier, inc=1, device_id={"coef": other}, device_id_type=MESH)

    snap = snap_ref[...]
    snap_t = snap.astype(F32).T.astype(jnp.bfloat16)
    gram = jnp.dot(snap_t, snap, preferred_element_type=F32)
    place = lax.broadcasted_iota(jnp.int32, (slab, slab), 0)
    one_hot = jnp.where(place == order_ref[...], 1.0, 0.0).astype(jnp.bfloat16)
    ordered_t = jnp.dot(snap_t, one_hot, preferred_element_type=F32)
    ordered = ordered_t.T
    for b in range(blocks):
        panels[blocks + b] = ordered[b * tile_rows : (b + 1) * tile_rows].astype(jnp.bfloat16)
    g_rows = rank // n
    for i in range(n):
        gsend[i] = gram[i * g_rows : (i + 1) * g_rows]

    @pl.when(me == 0)
    def _():
        for b in range(blocks):
            panels[b] = jnp.zeros(panels.shape[1:], panels.dtype)

    @pl.when(me == n - 1)
    def _():
        for b in range(blocks):
            panels[2 * blocks + b] = jnp.zeros(panels.shape[1:], panels.dtype)

    pl.semaphore_wait(barrier, n)

    def gram_part(slot, source, peer):
        return pltpu.make_async_remote_copy(
            src_ref=gsend.at[peer], dst_ref=grecv.at[source],
            send_sem=gs_sem.at[slot], recv_sem=gr_sem.at[source],
            device_id={"rows": peer}, device_id_type=MESH)

    peers(lambda d, peer: gram_part(d, me, peer).start())

    share = blocks // 2
    mine = half * share

    def halo(way, first_block, peer, to):
        return pltpu.make_async_remote_copy(
            src_ref=panels.at[pl.ds(first_block, share)], dst_ref=panels.at[pl.ds(to, share)],
            send_sem=hs_sem.at[way], recv_sem=hr_sem.at[way],
            device_id={"rows": peer}, device_id_type=MESH)

    def forward(way, base):
        place = pl.ds(base + mine, share)
        return pltpu.make_async_remote_copy(
            src_ref=panels.at[place], dst_ref=panels.at[place],
            send_sem=fs_sem.at[way], recv_sem=fr_sem.at[way],
            device_id={"coef": other}, device_id_type=MESH)

    up = halo(0, blocks + mine, jnp.minimum(me + 1, n - 1), mine)
    down = halo(1, blocks + mine, jnp.maximum(me - 1, 0), 2 * blocks + mine)

    @pl.when(me < n - 1)
    def _():
        up.start()

    @pl.when(me > 0)
    def _():
        down.start()

    coef_t = jnp.concatenate([coef_ref[...]] * (8 // ops), axis=0).T
    for k in range(ops):
        load[k].wait()
        for b in range(blocks):
            here = slice(b * tile_rows, (b + 1) * tile_rows)
            acc[k, here] = coef_t[here, k : k + 1] * ordered[here] + jnp.dot(
                tiles[k, b, 0], panels[blocks + b], preferred_element_type=F32)

    grecv[me] = gsend[me]
    peers(lambda d, peer: gram_part(d, peer, peer).wait_recv())
    gsum[...] = jnp.sum(grecv[...], axis=0)
    gall[me] = gsum[...]

    def gram_all(slot, source, peer):
        return pltpu.make_async_remote_copy(
            src_ref=gsum, dst_ref=gall.at[source],
            send_sem=as_sem.at[slot], recv_sem=ar_sem.at[source],
            device_id={"rows": peer}, device_id_type=MESH)

    peers(lambda d, peer: gram_all(d, me, peer).start())

    @pl.when(me > 0)
    def _():
        up.wait_recv()
        forward(0, 0).start()

    @pl.when(me < n - 1)
    def _():
        down.wait_recv()
        forward(1, 2 * blocks).start()

    @pl.when(me > 0)
    def _():
        forward(0, 0).wait()

    @pl.when(me < n - 1)
    def _():
        forward(1, 2 * blocks).wait()

    first = me * blocks - blocks
    weights = chebyshev(freq_ref[0])
    ordered_b = ordered_t.astype(jnp.bfloat16)
    weighted = jnp.zeros((slab, rank), F32)
    for k in range(ops):
        parts = []
        for b in range(blocks):
            here = slice(b * tile_rows, (b + 1) * tile_rows)
            total = acc[k, here]
            for j in range(1, per_row):
                at = jnp.clip(col_ref[k, b, j] - first, 0, 3 * blocks - 1)
                total = total + jnp.dot(tiles[k, b, j], panels[at], preferred_element_type=F32)
            parts.append(total.astype(jnp.bfloat16))
        image = jnp.concatenate(parts, axis=0)
        weight = jnp.where(half == 0, weights[k], weights[k + ops])
        weighted = weighted + weight * image.astype(F32)
        psend[k] = jnp.dot(ordered_b, image, preferred_element_type=F32)
    wsend[...] = weighted

    def projection_part(slot, source, peer):
        return pltpu.make_async_remote_copy(
            src_ref=psend.at[peer // per_op], dst_ref=precv.at[source],
            send_sem=ps_sem.at[slot], recv_sem=pr_sem.at[source],
            device_id={"rows": peer}, device_id_type=MESH)

    peers(lambda d, peer: projection_part(d, me, peer).start())
    swap = pltpu.make_async_remote_copy(
        src_ref=wsend, dst_ref=wrecv, send_sem=ws_sem, recv_sem=wr_sem,
        device_id={"coef": other}, device_id_type=MESH)
    swap.start()
    precv[me] = psend[me // per_op]

    peers(lambda d, peer: gram_all(d, peer, peer).wait_recv())
    inverse_factor(jnp.concatenate([gall[i] for i in range(n)], axis=0), w)
    for i in range(per_op):
        wt[i] = w[i * t_rows : (i + 1) * t_rows, :]

    swap.wait()
    both = (wsend[...] + wrecv[...]).T
    width = rank // 2
    sampled_ref[...] = jnp.where(half == 0, both[:width], both[width:]).astype(jnp.bfloat16)

    peers(lambda d, peer: projection_part(d, peer, peer).wait_recv())
    total = precv[0]
    if n <= 8:
        for i in range(1, n):
            total = total + precv[i]
    else:
        total = lax.fori_loop(1, n, lambda i, t: t + precv[i], total)
    inner = jnp.dot(wt[lax.rem(me, per_op)], total, preferred_element_type=F32, precision=HIGHEST)
    tsend[...] = lax.dot_general(
        inner, w[...], (((1,), (1,)), ((), ())), preferred_element_type=F32, precision=HIGHEST)
    tall[me] = tsend[...]

    def result_part(slot, source, peer):
        return pltpu.make_async_remote_copy(
            src_ref=tsend, dst_ref=tall.at[source],
            send_sem=ts_sem.at[slot], recv_sem=tr_sem.at[source],
            device_id={"rows": peer}, device_id_type=MESH)

    peers(lambda d, peer: result_part(d, me, peer).start())

    def sent(d, peer):
        gram_part(d, me, peer).wait_send()
        gram_all(d, me, peer).wait_send()
        projection_part(d, me, peer).wait_send()

    peers(sent)

    @pl.when(me < n - 1)
    def _():
        up.wait_send()

    @pl.when(me > 0)
    def _():
        down.wait_send()

    peers(lambda d, peer: result_part(d, peer, peer).wait_recv())
    for i in range(n):
        k, h = divmod(i, per_op)
        projected_ref[k, h * t_rows : (h + 1) * t_rows, :] = tall[i]
    peers(lambda d, peer: result_part(d, me, peer).wait_send())


def local(n, snapshots, panel_order, tile_values, self_coef, col_index, frequency):
    slab, rank = snapshots.shape
    ops, blocks, per_row, tile_rows = tile_values.shape[:4]
    t_rows = rank * ops // n
    vmem = pl.BlockSpec(memory_space=pltpu.VMEM)
    smem = pl.BlockSpec(memory_space=pltpu.SMEM)
    dma = pltpu.SemaphoreType.DMA
    sampled_t, projected = pl.pallas_call(
        functools.partial(kernel, n),
        out_shape=(
            jax.ShapeDtypeStruct((rank // 2, slab), jnp.bfloat16),
            jax.ShapeDtypeStruct((ops, rank, rank), F32),
        ),
        in_specs=[vmem, vmem, pl.BlockSpec(memory_space=pl.ANY), vmem, smem, smem],
        out_specs=(vmem, vmem),
        scratch_shapes=[
            pltpu.VMEM(tile_values.shape, jnp.bfloat16),
            pltpu.VMEM((3 * blocks, tile_rows, rank), jnp.bfloat16),
            pltpu.VMEM((ops, slab, rank), F32),
            pltpu.VMEM((n, rank // n, rank), F32),
            pltpu.VMEM((n, rank // n, rank), F32),
            pltpu.VMEM((rank // n, rank), F32),
            pltpu.VMEM((n, rank // n, rank), F32),
            pltpu.VMEM((rank, rank), F32),
            pltpu.VMEM((n // ops, t_rows, rank), F32),
            pltpu.VMEM((ops, rank, rank), F32),
            pltpu.VMEM((n, rank, rank), F32),
            pltpu.VMEM((t_rows, rank), F32),
            pltpu.VMEM((n, t_rows, rank), F32),
            pltpu.VMEM((slab, rank), F32),
            pltpu.VMEM((slab, rank), F32),
            dma((ops,)), dma((n,)), dma((n,)), dma((n,)), dma((n,)),
            dma((2,)), dma((2,)), dma((2,)), dma((2,)),
            dma((n,)), dma((n,)), dma((n,)), dma((n,)), dma, dma,
        ],
        compiler_params=pltpu.CompilerParams(
            collective_id=0, has_side_effects=True, vmem_limit_bytes=58 * 1024 * 1024),
        name="projection",
    )(snapshots, panel_order.reshape(1, slab), tile_values, self_coef, col_index, frequency)
    return sampled_t.T, projected


def solution(mesh):
    placed = (
        P(("sweep", "rows"), None),
        P(("sweep", "rows")),
        P(("sweep", "coef"), "rows", None, None, None),
        P(("sweep", "coef"), "rows"),
        P(("sweep", "coef"), "rows", None),
        P("sweep"),
    )
    return jax.shard_map(
        functools.partial(local, mesh.shape["rows"]),
        mesh=mesh,
        in_specs=placed,
        out_specs=(P(("sweep", "rows"), "coef"), P(("sweep", "coef"), None, None)),
        check_vma=False,
    )
```

```python
import functools

import jax
import jax.numpy as jnp
from jax import lax
from jax.experimental import pallas as pl
from jax.experimental.pallas import tpu as pltpu
from jax.sharding import PartitionSpec as P

K = 8
MESH = pl.DeviceIdType.MESH
HIGHEST = lax.Precision.HIGHEST
F32 = jnp.float32


def chebyshev(point):
    values = [jnp.float32(1.0), point]
    for _ in range(2, K):
        values.append(2.0 * point * values[-1] - values[-2])
    return values


def inverse_factor(a, w_ref):
    n = a.shape[0]
    row = lax.broadcasted_iota(jnp.int32, (n, n), 0)
    column = lax.broadcasted_iota(jnp.int32, (n, n), 1)
    right = jnp.where(row == column, 1.0, 0.0).astype(F32)
    rows8 = lax.broadcasted_iota(jnp.int32, (8, n), 0)
    for r0 in range(0, n, 8):
        rest = n - r0 - 8
        sa, sr, ta, tr = a[:8], right[:8], a[8:], right[8:]
        sc = [jnp.broadcast_to(sa[:, r0 + j : r0 + j + 1], (8, n)) for j in range(8)]
        if rest:
            tc = [jnp.broadcast_to(ta[:, r0 + j : r0 + j + 1], (rest, n)) for j in range(8)]
        scale = jnp.zeros((8, n), F32)
        for j in range(8):
            pivot = jnp.broadcast_to(sc[j][j : j + 1], (8, n))
            inverse = 1.0 / pivot
            factors = jnp.where(rows8 > j, sc[j] * inverse, 0.0)
            y = lax.rsqrt(pivot)
            y = y * (1.5 - 0.5 * pivot * y * y)
            scale = jnp.where(rows8 == j, y, scale)
            row_a, row_r = sa[j : j + 1], sr[j : j + 1]
            heads = [sc[i][j : j + 1] for i in range(8)]
            for i in range(j + 1, 8):
                sc[i] = sc[i] - factors * heads[i]
            sa = sa - factors * row_a
            sr = sr - factors * row_r
            if rest:
                below = tc[j] * inverse[:1]
                for i in range(j + 1, 8):
                    tc[i] = tc[i] - below * heads[i]
                ta = ta - below * row_a
                tr = tr - below * row_r
        w_ref[r0 : r0 + 8, :] = sr * scale
        a, right = ta, tr


def kernel(
    n, snap_ref, order_ref, tiles_ref, coef_ref, col_ref, freq_ref,
    sampled_ref, projected_ref,
    tiles, panels, acc, gsend, grecv, gsum, gall, w, terms, psend, precv, tsend, tall, wsend, wrecv,
    tile_sem, gs_sem, gr_sem, as_sem, ar_sem, hs_sem, hr_sem, fs_sem, fr_sem,
    ps_sem, pr_sem, ts_sem, tr_sem, ws_sem, wr_sem,
):
    me = lax.axis_index("rows")
    half = lax.axis_index("coef")
    other = 1 - half
    ops, blocks, per_row, tile_rows = tiles.shape[:4]
    slab, rank = snap_ref.shape
    per_op = n // ops
    t_rows = rank // per_op

    def peers(step):
        if n <= 8:
            for d in range(1, n):
                step(d, lax.rem(me + d, n))
        else:
            @pl.loop(1, n)
            def _(d):
                step(d, lax.rem(me + d, n))

    load = [
        pltpu.make_async_copy(tiles_ref.at[k], tiles.at[k], tile_sem.at[k]) for k in range(ops)
    ]
    for copy in load:
        copy.start()

    barrier = pltpu.get_barrier_semaphore()
    peers(lambda d, peer: pl.semaphore_signal(
        barrier, inc=1, device_id={"rows": peer}, device_id_type=MESH))
    pl.semaphore_signal(barrier, inc=1, device_id={"coef": other}, device_id_type=MESH)

    snap = snap_ref[...]
    snap_t = snap.astype(F32).T.astype(jnp.bfloat16)
    gram = jnp.dot(snap_t, snap, preferred_element_type=F32)
    place = lax.broadcasted_iota(jnp.int32, (slab, slab), 0)
    one_hot = jnp.where(place == order_ref[...], 1.0, 0.0).astype(jnp.bfloat16)
    ordered_t = jnp.dot(snap_t, one_hot, preferred_element_type=F32)
    ordered = ordered_t.T
    for b in range(blocks):
        panels[blocks + b] = ordered[b * tile_rows : (b + 1) * tile_rows].astype(jnp.bfloat16)
    g_rows = rank // n
    for i in range(n):
        gsend[i] = gram[i * g_rows : (i + 1) * g_rows]

    @pl.when(me == 0)
    def _():
        for b in range(blocks):
            panels[b] = jnp.zeros(panels.shape[1:], panels.dtype)

    @pl.when(me == n - 1)
    def _():
        for b in range(blocks):
            panels[2 * blocks + b] = jnp.zeros(panels.shape[1:], panels.dtype)

    pl.semaphore_wait(barrier, n)

    def gram_part(slot, source, peer):
        return pltpu.make_async_remote_copy(
            src_ref=gsend.at[peer], dst_ref=grecv.at[source],
            send_sem=gs_sem.at[slot], recv_sem=gr_sem.at[source],
            device_id={"rows": peer}, device_id_type=MESH)

    peers(lambda d, peer: gram_part(d, me, peer).start())

    share = blocks // 2
    mine = half * share

    def halo(way, first_block, peer, to):
        return pltpu.make_async_remote_copy(
            src_ref=panels.at[pl.ds(first_block, share)], dst_ref=panels.at[pl.ds(to, share)],
            send_sem=hs_sem.at[way], recv_sem=hr_sem.at[way],
            device_id={"rows": peer}, device_id_type=MESH)

    def forward(way, base):
        place = pl.ds(base + mine, share)
        return pltpu.make_async_remote_copy(
            src_ref=panels.at[place], dst_ref=panels.at[place],
            send_sem=fs_sem.at[way], recv_sem=fr_sem.at[way],
            device_id={"coef": other}, device_id_type=MESH)

    up = halo(0, blocks + mine, jnp.minimum(me + 1, n - 1), mine)
    down = halo(1, blocks + mine, jnp.maximum(me - 1, 0), 2 * blocks + mine)

    @pl.when(me < n - 1)
    def _():
        up.start()

    @pl.when(me > 0)
    def _():
        down.start()

    coef_t = jnp.concatenate([coef_ref[...]] * (8 // ops), axis=0).T
    for k in range(ops):
        load[k].wait()
        for b in range(blocks):
            here = slice(b * tile_rows, (b + 1) * tile_rows)
            acc[k, here] = coef_t[here, k : k + 1] * ordered[here] + jnp.dot(
                tiles[k, b, 0], panels[blocks + b], preferred_element_type=F32)

    grecv[me] = gsend[me]
    peers(lambda d, peer: gram_part(d, peer, peer).wait_recv())
    gsum[...] = jnp.sum(grecv[...], axis=0)
    gall[me] = gsum[...]

    def gram_all(slot, source, peer):
        return pltpu.make_async_remote_copy(
            src_ref=gsum, dst_ref=gall.at[source],
            send_sem=as_sem.at[slot], recv_sem=ar_sem.at[source],
            device_id={"rows": peer}, device_id_type=MESH)

    peers(lambda d, peer: gram_all(d, me, peer).start())

    @pl.when(me > 0)
    def _():
        up.wait_recv()
        forward(0, 0).start()

    @pl.when(me < n - 1)
    def _():
        down.wait_recv()
        forward(1, 2 * blocks).start()

    @pl.when(me > 0)
    def _():
        forward(0, 0).wait()

    @pl.when(me < n - 1)
    def _():
        forward(1, 2 * blocks).wait()

    first = me * blocks - blocks
    weights = chebyshev(freq_ref[0])
    ordered_b = ordered_t.astype(jnp.bfloat16)
    weighted = jnp.zeros((slab, rank), F32)
    for k in range(ops):
        parts = []
        for b in range(blocks):
            here = slice(b * tile_rows, (b + 1) * tile_rows)
            total = acc[k, here]
            for j in range(1, per_row):
                at = jnp.clip(col_ref[k, b, j] - first, 0, 3 * blocks - 1)
                total = total + jnp.dot(tiles[k, b, j], panels[at], preferred_element_type=F32)
            parts.append(total.astype(jnp.bfloat16))
        image = jnp.concatenate(parts, axis=0)
        weight = jnp.where(half == 0, weights[k], weights[k + ops])
        weighted = weighted + weight * image.astype(F32)
        terms[k] = jnp.dot(ordered_b, image, preferred_element_type=F32)
    wsend[...] = weighted
    swap = pltpu.make_async_remote_copy(
        src_ref=wsend, dst_ref=wrecv, send_sem=ws_sem, recv_sem=wr_sem,
        device_id={"coef": other}, device_id_type=MESH)
    swap.start()

    peers(lambda d, peer: gram_all(d, peer, peer).wait_recv())
    inverse_factor(jnp.concatenate([gall[i] for i in range(n)], axis=0), w)

    inverse = w[...]
    inner = jnp.dot(
        inverse, jnp.concatenate([terms[k] for k in range(ops)], axis=1),
        preferred_element_type=F32, precision=HIGHEST)
    for k in range(ops):
        projected = lax.dot_general(
            inner[:, k * rank : (k + 1) * rank], inverse, (((1,), (1,)), ((), ())),
            preferred_element_type=F32, precision=HIGHEST)
        for h in range(per_op):
            psend[k * per_op + h] = projected[h * t_rows : (h + 1) * t_rows].astype(psend.dtype)

    def projection_part(slot, source, peer):
        return pltpu.make_async_remote_copy(
            src_ref=psend.at[peer], dst_ref=precv.at[source],
            send_sem=ps_sem.at[slot], recv_sem=pr_sem.at[source],
            device_id={"rows": peer}, device_id_type=MESH)

    peers(lambda d, peer: projection_part(d, me, peer).start())
    precv[me] = psend[me]

    swap.wait()
    both = (wsend[...] + wrecv[...]).T
    width = rank // 2
    sampled_ref[...] = jnp.where(half == 0, both[:width], both[width:])

    peers(lambda d, peer: projection_part(d, peer, peer).wait_recv())
    total = precv[0].astype(F32)
    if n <= 8:
        for i in range(1, n):
            total = total + precv[i].astype(F32)
    else:
        total = lax.fori_loop(1, n, lambda i, t: t + precv[i].astype(F32), total)
    tsend[...] = total.astype(tsend.dtype)
    tall[me] = tsend[...]

    def result_part(slot, source, peer):
        return pltpu.make_async_remote_copy(
            src_ref=tsend, dst_ref=tall.at[source],
            send_sem=ts_sem.at[slot], recv_sem=tr_sem.at[source],
            device_id={"rows": peer}, device_id_type=MESH)

    peers(lambda d, peer: result_part(d, me, peer).start())

    def sent(d, peer):
        gram_part(d, me, peer).wait_send()
        gram_all(d, me, peer).wait_send()
        projection_part(d, me, peer).wait_send()

    peers(sent)

    @pl.when(me < n - 1)
    def _():
        up.wait_send()

    @pl.when(me > 0)
    def _():
        down.wait_send()

    peers(lambda d, peer: result_part(d, peer, peer).wait_recv())
    projected_ref[...] = tall[...]
    peers(lambda d, peer: result_part(d, me, peer).wait_send())


def local(n, snapshots, panel_order, tile_values, self_coef, col_index, frequency):
    slab, rank = snapshots.shape
    ops, blocks, per_row, tile_rows = tile_values.shape[:4]
    t_rows = rank * ops // n
    wire = jnp.bfloat16 if t_rows % 16 == 0 else F32
    vmem = pl.BlockSpec(memory_space=pltpu.VMEM)
    smem = pl.BlockSpec(memory_space=pltpu.SMEM)
    dma = pltpu.SemaphoreType.DMA
    sampled_t, projected = pl.pallas_call(
        functools.partial(kernel, n),
        out_shape=(
            jax.ShapeDtypeStruct((rank // 2, slab), F32),
            jax.ShapeDtypeStruct((n, t_rows, rank), wire),
        ),
        in_specs=[vmem, vmem, pl.BlockSpec(memory_space=pl.ANY), vmem, smem, smem],
        out_specs=(vmem, vmem),
        scratch_shapes=[
            pltpu.VMEM(tile_values.shape, jnp.bfloat16),
            pltpu.VMEM((3 * blocks, tile_rows, rank), jnp.bfloat16),
            pltpu.VMEM((ops, slab, rank), F32),
            pltpu.VMEM((n, rank // n, rank), F32),
            pltpu.VMEM((n, rank // n, rank), F32),
            pltpu.VMEM((rank // n, rank), F32),
            pltpu.VMEM((n, rank // n, rank), F32),
            pltpu.VMEM((rank, rank), F32),
            pltpu.VMEM((ops, rank, rank), F32),
            pltpu.VMEM((n, t_rows, rank), wire),
            pltpu.VMEM((n, t_rows, rank), wire),
            pltpu.VMEM((t_rows, rank), wire),
            pltpu.VMEM((n, t_rows, rank), wire),
            pltpu.VMEM((slab, rank), F32),
            pltpu.VMEM((slab, rank), F32),
            dma((ops,)), dma((n,)), dma((n,)), dma((n,)), dma((n,)),
            dma((2,)), dma((2,)), dma((2,)), dma((2,)),
            dma((n,)), dma((n,)), dma((n,)), dma((n,)), dma, dma,
        ],
        compiler_params=pltpu.CompilerParams(
            collective_id=0, has_side_effects=True, vmem_limit_bytes=58 * 1024 * 1024),
        name="projection",
    )(snapshots, panel_order.reshape(1, slab), tile_values, self_coef, col_index, frequency)
    return sampled_t.T.astype(jnp.bfloat16), projected.reshape(ops, rank, rank).astype(F32)


def solution(mesh):
    placed = (
        P(("sweep", "rows"), None),
        P(("sweep", "rows")),
        P(("sweep", "coef"), "rows", None, None, None),
        P(("sweep", "coef"), "rows"),
        P(("sweep", "coef"), "rows", None),
        P("sweep"),
    )
    return jax.shard_map(
        functools.partial(local, mesh.shape["rows"]),
        mesh=mesh,
        in_specs=placed,
        out_specs=(P(("sweep", "rows"), "coef"), P(("sweep", "coef"), None, None)),
        check_vma=False,
    )
```

```python
import functools

import jax
import jax.numpy as jnp
from jax import lax
from jax.experimental import pallas as pl
from jax.experimental.pallas import tpu as pltpu
from jax.sharding import PartitionSpec as P

K = 8
MESH = pl.DeviceIdType.MESH
HIGHEST = lax.Precision.HIGHEST
F32 = jnp.float32


def chebyshev(point):
    values = [jnp.float32(1.0), point]
    for _ in range(2, K):
        values.append(2.0 * point * values[-1] - values[-2])
    return values


def inverse_factor(a, w_ref):
    n = a.shape[0]
    row = lax.broadcasted_iota(jnp.int32, (n, n), 0)
    column = lax.broadcasted_iota(jnp.int32, (n, n), 1)
    right = jnp.where(row == column, 1.0, 0.0).astype(F32)
    rows8 = lax.broadcasted_iota(jnp.int32, (8, n), 0)
    for r0 in range(0, n, 8):
        rest = n - r0 - 8
        sa, sr, ta, tr = a[:8], right[:8], a[8:], right[8:]
        sc = [jnp.broadcast_to(sa[:, r0 + j : r0 + j + 1], (8, n)) for j in range(8)]
        if rest:
            tc = [jnp.broadcast_to(ta[:, r0 + j : r0 + j + 1], (rest, n)) for j in range(8)]
        scale = jnp.zeros((8, n), F32)
        for j in range(8):
            pivot = jnp.broadcast_to(sc[j][j : j + 1], (8, n))
            inverse = 1.0 / pivot
            factors = jnp.where(rows8 > j, sc[j] * inverse, 0.0)
            y = lax.rsqrt(pivot)
            y = y * (1.5 - 0.5 * pivot * y * y)
            scale = jnp.where(rows8 == j, y, scale)
            row_a, row_r = sa[j : j + 1], sr[j : j + 1]
            heads = [sc[i][j : j + 1] for i in range(8)]
            for i in range(j + 1, 8):
                sc[i] = sc[i] - factors * heads[i]
            sa = sa - factors * row_a
            sr = sr - factors * row_r
            if rest:
                below = tc[j] * inverse[:1]
                for i in range(j + 1, 8):
                    tc[i] = tc[i] - below * heads[i]
                ta = ta - below * row_a
                tr = tr - below * row_r
        w_ref[r0 : r0 + 8, :] = sr * scale
        a, right = ta, tr


def kernel(
    n, snap_ref, order_ref, tiles_ref, coef_ref, col_ref, freq_ref,
    sampled_ref, projected_ref,
    tiles, panels, acc, gsend, grecv, gsum, gall, w, terms, psend, precv, tsend, tall, wsend, wrecv,
    tile_sem, gs_sem, gr_sem, as_sem, ar_sem, hs_sem, hr_sem, fs_sem, fr_sem,
    ps_sem, pr_sem, ts_sem, tr_sem, ws_sem, wr_sem,
):
    me = lax.axis_index("rows")
    half = lax.axis_index("coef")
    other = 1 - half
    ops, blocks, per_row, tile_rows = tiles.shape[:4]
    slab, rank = snap_ref.shape
    per_op = n // ops
    t_rows = rank // per_op

    def peers(step):
        if n <= 8:
            for d in range(1, n):
                step(d, lax.rem(me + d, n))
        else:
            @pl.loop(1, n)
            def _(d):
                step(d, lax.rem(me + d, n))

    load = [
        pltpu.make_async_copy(tiles_ref.at[k], tiles.at[k], tile_sem.at[k]) for k in range(ops)
    ]
    for copy in load:
        copy.start()

    barrier = pltpu.get_barrier_semaphore()
    peers(lambda d, peer: pl.semaphore_signal(
        barrier, inc=1, device_id={"rows": peer}, device_id_type=MESH))
    pl.semaphore_signal(barrier, inc=1, device_id={"coef": other}, device_id_type=MESH)

    snap = snap_ref[...]
    snap_t = snap.astype(F32).T.astype(jnp.bfloat16)
    gram = jnp.dot(snap_t, snap, preferred_element_type=F32)
    g_rows = rank // n
    for i in range(n):
        gsend[i] = gram[i * g_rows : (i + 1) * g_rows]

    pl.semaphore_wait(barrier, n)

    def gram_part(slot, source, peer):
        return pltpu.make_async_remote_copy(
            src_ref=gsend.at[peer], dst_ref=grecv.at[source],
            send_sem=gs_sem.at[slot], recv_sem=gr_sem.at[source],
            device_id={"rows": peer}, device_id_type=MESH)

    peers(lambda d, peer: gram_part(d, me, peer).start())

    place = lax.broadcasted_iota(jnp.int32, (slab, slab), 0)
    one_hot = jnp.where(place == order_ref[...], 1.0, 0.0).astype(jnp.bfloat16)
    ordered_t = jnp.dot(snap_t, one_hot, preferred_element_type=F32)
    ordered = ordered_t.T
    for b in range(blocks):
        panels[blocks + b] = ordered[b * tile_rows : (b + 1) * tile_rows].astype(jnp.bfloat16)
    @pl.when(me == 0)
    def _():
        for b in range(blocks):
            panels[b] = jnp.zeros(panels.shape[1:], panels.dtype)

    @pl.when(me == n - 1)
    def _():
        for b in range(blocks):
            panels[2 * blocks + b] = jnp.zeros(panels.shape[1:], panels.dtype)

    share = blocks // 2
    mine = half * share

    def halo(way, first_block, peer, to):
        return pltpu.make_async_remote_copy(
            src_ref=panels.at[pl.ds(first_block, share)], dst_ref=panels.at[pl.ds(to, share)],
            send_sem=hs_sem.at[way], recv_sem=hr_sem.at[way],
            device_id={"rows": peer}, device_id_type=MESH)

    def forward(way, base):
        place = pl.ds(base + mine, share)
        return pltpu.make_async_remote_copy(
            src_ref=panels.at[place], dst_ref=panels.at[place],
            send_sem=fs_sem.at[way], recv_sem=fr_sem.at[way],
            device_id={"coef": other}, device_id_type=MESH)

    up = halo(0, blocks + mine, jnp.minimum(me + 1, n - 1), mine)
    down = halo(1, blocks + mine, jnp.maximum(me - 1, 0), 2 * blocks + mine)

    @pl.when(me < n - 1)
    def _():
        up.start()

    @pl.when(me > 0)
    def _():
        down.start()

    coef_t = jnp.concatenate([coef_ref[...]] * (8 // ops), axis=0).T
    for k in range(ops):
        load[k].wait()
        for b in range(blocks):
            here = slice(b * tile_rows, (b + 1) * tile_rows)
            acc[k, here] = coef_t[here, k : k + 1] * ordered[here] + jnp.dot(
                tiles[k, b, 0], panels[blocks + b], preferred_element_type=F32)

    grecv[me] = gsend[me]
    peers(lambda d, peer: gram_part(d, peer, peer).wait_recv())
    gsum[...] = jnp.sum(grecv[...], axis=0)
    gall[me] = gsum[...]

    def gram_all(slot, source, peer):
        return pltpu.make_async_remote_copy(
            src_ref=gsum, dst_ref=gall.at[source],
            send_sem=as_sem.at[slot], recv_sem=ar_sem.at[source],
            device_id={"rows": peer}, device_id_type=MESH)

    peers(lambda d, peer: gram_all(d, me, peer).start())

    @pl.when(me > 0)
    def _():
        up.wait_recv()
        forward(0, 0).start()

    @pl.when(me < n - 1)
    def _():
        down.wait_recv()
        forward(1, 2 * blocks).start()

    @pl.when(me > 0)
    def _():
        forward(0, 0).wait()

    @pl.when(me < n - 1)
    def _():
        forward(1, 2 * blocks).wait()

    first = me * blocks - blocks
    weights = chebyshev(freq_ref[0])
    ordered_b = ordered_t.astype(jnp.bfloat16)
    weighted = jnp.zeros((slab, rank), F32)
    for k in range(ops):
        parts = []
        for b in range(blocks):
            here = slice(b * tile_rows, (b + 1) * tile_rows)
            total = acc[k, here]
            for j in range(1, per_row):
                at = jnp.clip(col_ref[k, b, j] - first, 0, 3 * blocks - 1)
                total = total + jnp.dot(tiles[k, b, j], panels[at], preferred_element_type=F32)
            parts.append(total.astype(jnp.bfloat16))
        image = jnp.concatenate(parts, axis=0)
        weight = jnp.where(half == 0, weights[k], weights[k + ops])
        weighted = weighted + weight * image.astype(F32)
        terms[k] = jnp.dot(ordered_b, image, preferred_element_type=F32)
    wsend[...] = weighted
    swap = pltpu.make_async_remote_copy(
        src_ref=wsend, dst_ref=wrecv, send_sem=ws_sem, recv_sem=wr_sem,
        device_id={"coef": other}, device_id_type=MESH)
    swap.start()

    peers(lambda d, peer: gram_all(d, peer, peer).wait_recv())
    inverse_factor(jnp.concatenate([gall[i] for i in range(n)], axis=0), w)

    def projection_part(slot, source, peer):
        return pltpu.make_async_remote_copy(
            src_ref=psend.at[peer], dst_ref=precv.at[source],
            send_sem=ps_sem.at[slot], recv_sem=pr_sem.at[source],
            device_id={"rows": peer}, device_id_type=MESH)

    inverse = w[...]
    for s in range(1, ops + 1):
        k = lax.rem(me // per_op + s, ops)
        inner = jnp.dot(inverse, terms[k], preferred_element_type=F32, precision=HIGHEST)
        projected = lax.dot_general(
            inner, inverse, (((1,), (1,)), ((), ())),
            preferred_element_type=F32, precision=HIGHEST)
        for h in range(per_op):
            psend[k * per_op + h] = projected[h * t_rows : (h + 1) * t_rows].astype(psend.dtype)
        for h in range(per_op):
            peer = k * per_op + h

            @pl.when(peer != me)
            def _():
                projection_part(peer, me, peer).start()

    precv[me] = psend[me]

    swap.wait()
    both = (wsend[...] + wrecv[...]).T
    width = rank // 2
    sampled_ref[...] = jnp.where(half == 0, both[:width], both[width:])

    peers(lambda d, peer: projection_part(d, peer, peer).wait_recv())
    total = precv[0].astype(F32)
    if n <= 8:
        for i in range(1, n):
            total = total + precv[i].astype(F32)
    else:
        total = lax.fori_loop(1, n, lambda i, t: t + precv[i].astype(F32), total)
    tsend[...] = total.astype(tsend.dtype)
    tall[me] = tsend[...]

    def result_part(slot, source, peer):
        return pltpu.make_async_remote_copy(
            src_ref=tsend, dst_ref=tall.at[source],
            send_sem=ts_sem.at[slot], recv_sem=tr_sem.at[source],
            device_id={"rows": peer}, device_id_type=MESH)

    peers(lambda d, peer: result_part(d, me, peer).start())

    def sent(d, peer):
        gram_part(d, me, peer).wait_send()
        gram_all(d, me, peer).wait_send()
        projection_part(peer, me, peer).wait_send()

    peers(sent)

    @pl.when(me < n - 1)
    def _():
        up.wait_send()

    @pl.when(me > 0)
    def _():
        down.wait_send()

    peers(lambda d, peer: result_part(d, peer, peer).wait_recv())
    projected_ref[...] = tall[...]
    peers(lambda d, peer: result_part(d, me, peer).wait_send())


def finish(sampled_ref, projected_ref, sampled_out, projected_out):
    sampled_out[...] = sampled_ref[...].astype(sampled_out.dtype)
    projected_out[...] = projected_ref[...].astype(projected_out.dtype)


def local(n, snapshots, panel_order, tile_values, self_coef, col_index, frequency):
    slab, rank = snapshots.shape
    ops, blocks, per_row, tile_rows = tile_values.shape[:4]
    t_rows = rank * ops // n
    wire = jnp.bfloat16 if t_rows % 16 == 0 else F32
    vmem = pl.BlockSpec(memory_space=pltpu.VMEM)
    smem = pl.BlockSpec(memory_space=pltpu.SMEM)
    dma = pltpu.SemaphoreType.DMA
    sampled_t, projected = pl.pallas_call(
        functools.partial(kernel, n),
        out_shape=(
            jax.ShapeDtypeStruct((rank // 2, slab), F32),
            jax.ShapeDtypeStruct((n, t_rows, rank), wire),
        ),
        in_specs=[vmem, vmem, pl.BlockSpec(memory_space=pl.ANY), vmem, smem, smem],
        out_specs=(vmem, vmem),
        scratch_shapes=[
            pltpu.VMEM(tile_values.shape, jnp.bfloat16),
            pltpu.VMEM((3 * blocks, tile_rows, rank), jnp.bfloat16),
            pltpu.VMEM((ops, slab, rank), F32),
            pltpu.VMEM((n, rank // n, rank), F32),
            pltpu.VMEM((n, rank // n, rank), F32),
            pltpu.VMEM((rank // n, rank), F32),
            pltpu.VMEM((n, rank // n, rank), F32),
            pltpu.VMEM((rank, rank), F32),
            pltpu.VMEM((ops, rank, rank), F32),
            pltpu.VMEM((n, t_rows, rank), wire),
            pltpu.VMEM((n, t_rows, rank), wire),
            pltpu.VMEM((t_rows, rank), wire),
            pltpu.VMEM((n, t_rows, rank), wire),
            pltpu.VMEM((slab, rank), F32),
            pltpu.VMEM((slab, rank), F32),
            dma((ops,)), dma((n,)), dma((n,)), dma((n,)), dma((n,)),
            dma((2,)), dma((2,)), dma((2,)), dma((2,)),
            dma((n,)), dma((n,)), dma((n,)), dma((n,)), dma, dma,
        ],
        compiler_params=pltpu.CompilerParams(
            collective_id=0, has_side_effects=True, vmem_limit_bytes=58 * 1024 * 1024),
        name="projection",
    )(snapshots, panel_order.reshape(1, slab), tile_values, self_coef, col_index, frequency)
    sampled_t, projected = pl.pallas_call(
        finish,
        out_shape=(
            jax.ShapeDtypeStruct(sampled_t.shape, jnp.bfloat16),
            jax.ShapeDtypeStruct(projected.shape, F32),
        ),
        name="finish",
    )(sampled_t, projected)
    return sampled_t.T, projected.reshape(ops, rank, rank)


def solution(mesh):
    placed = (
        P(("sweep", "rows"), None),
        P(("sweep", "rows")),
        P(("sweep", "coef"), "rows", None, None, None),
        P(("sweep", "coef"), "rows"),
        P(("sweep", "coef"), "rows", None),
        P("sweep"),
    )
    return jax.shard_map(
        functools.partial(local, mesh.shape["rows"]),
        mesh=mesh,
        in_specs=placed,
        out_specs=(P(("sweep", "rows"), "coef"), P(("sweep", "coef"), None, None)),
        check_vma=False,
    )
```

```python
import functools

import jax
import jax.numpy as jnp
from jax import lax
from jax.experimental import pallas as pl
from jax.experimental.pallas import tpu as pltpu
from jax.sharding import PartitionSpec as P

K = 8
MESH = pl.DeviceIdType.MESH
HIGHEST = lax.Precision.HIGHEST
F32 = jnp.float32


def chebyshev(point):
    values = [jnp.float32(1.0), point]
    for _ in range(2, K):
        values.append(2.0 * point * values[-1] - values[-2])
    return values


def inverse_factor(a, w_ref):
    n = a.shape[0]
    row = lax.broadcasted_iota(jnp.int32, (n, n), 0)
    column = lax.broadcasted_iota(jnp.int32, (n, n), 1)
    right = jnp.where(row == column, 1.0, 0.0).astype(F32)
    rows8 = lax.broadcasted_iota(jnp.int32, (8, n), 0)
    for r0 in range(0, n, 8):
        rest = n - r0 - 8
        sa, sr, ta, tr = a[:8], right[:8], a[8:], right[8:]
        sc = [jnp.broadcast_to(sa[:, r0 + j : r0 + j + 1], (8, n)) for j in range(8)]
        if rest:
            tc = [jnp.broadcast_to(ta[:, r0 + j : r0 + j + 1], (rest, n)) for j in range(8)]
        scale = jnp.zeros((8, n), F32)
        for j in range(8):
            pivot = jnp.broadcast_to(sc[j][j : j + 1], (8, n))
            inverse = 1.0 / pivot
            factors = jnp.where(rows8 > j, sc[j] * inverse, 0.0)
            y = lax.rsqrt(pivot)
            y = y * (1.5 - 0.5 * pivot * y * y)
            scale = jnp.where(rows8 == j, y, scale)
            row_a, row_r = sa[j : j + 1], sr[j : j + 1]
            heads = [sc[i][j : j + 1] for i in range(8)]
            for i in range(j + 1, 8):
                sc[i] = sc[i] - factors * heads[i]
            sa = sa - factors * row_a
            sr = sr - factors * row_r
            if rest:
                below = tc[j] * inverse[:1]
                for i in range(j + 1, 8):
                    tc[i] = tc[i] - below * heads[i]
                ta = ta - below * row_a
                tr = tr - below * row_r
        w_ref[r0 : r0 + 8, :] = sr * scale
        a, right = ta, tr


def kernel(
    n, snap_ref, order_ref, tiles_ref, coef_ref, col_ref, freq_ref,
    sampled_ref, projected_ref,
    tiles, panels, acc, gsend, grecv, gsum, gall, w, terms, psend, precv, tsend, tall, wsend, wrecv,
    tile_sem, gs_sem, gr_sem, as_sem, ar_sem, hs_sem, hr_sem, fs_sem, fr_sem,
    ps_sem, pr_sem, ts_sem, tr_sem, ws_sem, wr_sem,
):
    me = lax.axis_index("rows")
    half = lax.axis_index("coef")
    other = 1 - half
    ops, blocks, per_row, tile_rows = tiles.shape[:4]
    slab, rank = snap_ref.shape
    per_op = n // ops
    t_rows = rank // per_op

    def peers(step):
        if n <= 8:
            for d in range(1, n):
                step(d, lax.rem(me + d, n))
        else:
            @pl.loop(1, n)
            def _(d):
                step(d, lax.rem(me + d, n))

    load = [
        pltpu.make_async_copy(tiles_ref.at[k], tiles.at[k], tile_sem.at[k]) for k in range(ops)
    ]
    for copy in load:
        copy.start()

    barrier = pltpu.get_barrier_semaphore()
    peers(lambda d, peer: pl.semaphore_signal(
        barrier, inc=1, device_id={"rows": peer}, device_id_type=MESH))
    pl.semaphore_signal(barrier, inc=1, device_id={"coef": other}, device_id_type=MESH)

    snap = snap_ref[...]
    snap_t = snap.astype(F32).T.astype(jnp.bfloat16)
    gram = jnp.dot(snap_t, snap, preferred_element_type=F32)
    g_rows = rank // n
    for i in range(n):
        gsend[i] = gram[i * g_rows : (i + 1) * g_rows]

    pl.semaphore_wait(barrier, n)

    def gram_part(slot, source, peer):
        return pltpu.make_async_remote_copy(
            src_ref=gsend.at[peer], dst_ref=grecv.at[source],
            send_sem=gs_sem.at[slot], recv_sem=gr_sem.at[source],
            device_id={"rows": peer}, device_id_type=MESH)

    peers(lambda d, peer: gram_part(d, me, peer).start())

    place = lax.broadcasted_iota(jnp.int32, (slab, slab), 0)
    one_hot = jnp.where(place == order_ref[...], 1.0, 0.0).astype(jnp.bfloat16)
    ordered_t = jnp.dot(snap_t, one_hot, preferred_element_type=F32)
    ordered = ordered_t.T
    for b in range(blocks):
        panels[blocks + b] = ordered[b * tile_rows : (b + 1) * tile_rows].astype(jnp.bfloat16)
    @pl.when(me == 0)
    def _():
        for b in range(blocks):
            panels[b] = jnp.zeros(panels.shape[1:], panels.dtype)

    @pl.when(me == n - 1)
    def _():
        for b in range(blocks):
            panels[2 * blocks + b] = jnp.zeros(panels.shape[1:], panels.dtype)

    share = blocks // 2
    mine = half * share

    def halo(way, first_block, peer, to):
        return pltpu.make_async_remote_copy(
            src_ref=panels.at[pl.ds(first_block, share)], dst_ref=panels.at[pl.ds(to, share)],
            send_sem=hs_sem.at[way], recv_sem=hr_sem.at[way],
            device_id={"rows": peer}, device_id_type=MESH)

    def forward(way, base):
        place = pl.ds(base + mine, share)
        return pltpu.make_async_remote_copy(
            src_ref=panels.at[place], dst_ref=panels.at[place],
            send_sem=fs_sem.at[way], recv_sem=fr_sem.at[way],
            device_id={"coef": other}, device_id_type=MESH)

    up = halo(0, blocks + mine, jnp.minimum(me + 1, n - 1), mine)
    down = halo(1, blocks + mine, jnp.maximum(me - 1, 0), 2 * blocks + mine)

    @pl.when(me < n - 1)
    def _():
        up.start()

    @pl.when(me > 0)
    def _():
        down.start()

    coef_t = jnp.concatenate([coef_ref[...]] * (8 // ops), axis=0).T
    for k in range(ops):
        load[k].wait()
        for b in range(blocks):
            here = slice(b * tile_rows, (b + 1) * tile_rows)
            acc[k, here] = coef_t[here, k : k + 1] * ordered[here] + jnp.dot(
                tiles[k, b, 0], panels[blocks + b], preferred_element_type=F32)

    grecv[me] = gsend[me]
    peers(lambda d, peer: gram_part(d, peer, peer).wait_recv())
    gsum[...] = jnp.sum(grecv[...], axis=0)
    gall[me] = gsum[...]

    def gram_all(slot, source, peer):
        return pltpu.make_async_remote_copy(
            src_ref=gsum, dst_ref=gall.at[source],
            send_sem=as_sem.at[slot], recv_sem=ar_sem.at[source],
            device_id={"rows": peer}, device_id_type=MESH)

    peers(lambda d, peer: gram_all(d, me, peer).start())

    @pl.when(me > 0)
    def _():
        up.wait_recv()
        forward(0, 0).start()

    @pl.when(me < n - 1)
    def _():
        down.wait_recv()
        forward(1, 2 * blocks).start()

    @pl.when(me > 0)
    def _():
        forward(0, 0).wait()

    @pl.when(me < n - 1)
    def _():
        forward(1, 2 * blocks).wait()

    first = me * blocks - blocks
    weights = chebyshev(freq_ref[0])
    ordered_b = ordered_t.astype(jnp.bfloat16)
    weighted = jnp.zeros((slab, rank), F32)
    for k in range(ops):
        parts = []
        for b in range(blocks):
            here = slice(b * tile_rows, (b + 1) * tile_rows)
            total = acc[k, here]
            for j in range(1, per_row):
                at = jnp.clip(col_ref[k, b, j] - first, 0, 3 * blocks - 1)
                total = total + jnp.dot(tiles[k, b, j], panels[at], preferred_element_type=F32)
            parts.append(total.astype(jnp.bfloat16))
        image = jnp.concatenate(parts, axis=0)
        weight = jnp.where(half == 0, weights[k], weights[k + ops])
        weighted = weighted + weight * image.astype(F32)
        terms[k] = jnp.dot(ordered_b, image, preferred_element_type=F32)
    wsend[...] = weighted
    swap = pltpu.make_async_remote_copy(
        src_ref=wsend, dst_ref=wrecv, send_sem=ws_sem, recv_sem=wr_sem,
        device_id={"coef": other}, device_id_type=MESH)
    swap.start()

    peers(lambda d, peer: gram_all(d, peer, peer).wait_recv())
    inverse_factor(jnp.concatenate([gall[i] for i in range(n)], axis=0), w)

    def projection_part(slot, source, peer):
        return pltpu.make_async_remote_copy(
            src_ref=psend.at[peer], dst_ref=precv.at[source],
            send_sem=ps_sem.at[slot], recv_sem=pr_sem.at[source],
            device_id={"rows": peer}, device_id_type=MESH)

    inverse = w[...]
    for s in range(1, ops + 1):
        k = s - 1
        inner = jnp.dot(inverse, terms[k], preferred_element_type=F32, precision=HIGHEST)
        projected = lax.dot_general(
            inner, inverse, (((1,), (1,)), ((), ())),
            preferred_element_type=F32, precision=HIGHEST)
        for h in range(per_op):
            psend[k * per_op + h] = projected[h * t_rows : (h + 1) * t_rows].astype(psend.dtype)

    peers(lambda d, peer: projection_part(peer, me, peer).start())
    precv[me] = psend[me]

    swap.wait()
    both = (wsend[...] + wrecv[...]).T
    width = rank // 2
    sampled_ref[...] = jnp.where(half == 0, both[:width], both[width:])

    peers(lambda d, peer: projection_part(d, peer, peer).wait_recv())
    total = precv[0].astype(F32)
    if n <= 8:
        for i in range(1, n):
            total = total + precv[i].astype(F32)
    else:
        total = lax.fori_loop(1, n, lambda i, t: t + precv[i].astype(F32), total)
    tsend[...] = total.astype(tsend.dtype)
    tall[me] = tsend[...]

    def result_part(slot, source, peer):
        return pltpu.make_async_remote_copy(
            src_ref=tsend, dst_ref=tall.at[source],
            send_sem=ts_sem.at[slot], recv_sem=tr_sem.at[source],
            device_id={"rows": peer}, device_id_type=MESH)

    peers(lambda d, peer: result_part(d, me, peer).start())

    def sent(d, peer):
        gram_part(d, me, peer).wait_send()
        gram_all(d, me, peer).wait_send()
        projection_part(peer, me, peer).wait_send()

    peers(sent)

    @pl.when(me < n - 1)
    def _():
        up.wait_send()

    @pl.when(me > 0)
    def _():
        down.wait_send()

    peers(lambda d, peer: result_part(d, peer, peer).wait_recv())
    projected_ref[...] = tall[...]
    peers(lambda d, peer: result_part(d, me, peer).wait_send())


def finish(sampled_ref, projected_ref, sampled_out, projected_out):
    sampled_out[...] = sampled_ref[...].astype(sampled_out.dtype)
    projected_out[...] = projected_ref[...].astype(projected_out.dtype)


def local(n, snapshots, panel_order, tile_values, self_coef, col_index, frequency):
    slab, rank = snapshots.shape
    ops, blocks, per_row, tile_rows = tile_values.shape[:4]
    t_rows = rank * ops // n
    wire = jnp.bfloat16 if t_rows % 16 == 0 else F32
    vmem = pl.BlockSpec(memory_space=pltpu.VMEM)
    smem = pl.BlockSpec(memory_space=pltpu.SMEM)
    dma = pltpu.SemaphoreType.DMA
    sampled_t, projected = pl.pallas_call(
        functools.partial(kernel, n),
        out_shape=(
            jax.ShapeDtypeStruct((rank // 2, slab), F32),
            jax.ShapeDtypeStruct((n, t_rows, rank), wire),
        ),
        in_specs=[vmem, vmem, pl.BlockSpec(memory_space=pl.ANY), vmem, smem, smem],
        out_specs=(vmem, vmem),
        scratch_shapes=[
            pltpu.VMEM(tile_values.shape, jnp.bfloat16),
            pltpu.VMEM((3 * blocks, tile_rows, rank), jnp.bfloat16),
            pltpu.VMEM((ops, slab, rank), F32),
            pltpu.VMEM((n, rank // n, rank), F32),
            pltpu.VMEM((n, rank // n, rank), F32),
            pltpu.VMEM((rank // n, rank), F32),
            pltpu.VMEM((n, rank // n, rank), F32),
            pltpu.VMEM((rank, rank), F32),
            pltpu.VMEM((ops, rank, rank), F32),
            pltpu.VMEM((n, t_rows, rank), wire),
            pltpu.VMEM((n, t_rows, rank), wire),
            pltpu.VMEM((t_rows, rank), wire),
            pltpu.VMEM((n, t_rows, rank), wire),
            pltpu.VMEM((slab, rank), F32),
            pltpu.VMEM((slab, rank), F32),
            dma((ops,)), dma((n,)), dma((n,)), dma((n,)), dma((n,)),
            dma((2,)), dma((2,)), dma((2,)), dma((2,)),
            dma((n,)), dma((n,)), dma((n,)), dma((n,)), dma, dma,
        ],
        compiler_params=pltpu.CompilerParams(
            collective_id=0, has_side_effects=True, vmem_limit_bytes=58 * 1024 * 1024),
        name="projection",
    )(snapshots, panel_order.reshape(1, slab), tile_values, self_coef, col_index, frequency)
    sampled_t, projected = pl.pallas_call(
        finish,
        out_shape=(
            jax.ShapeDtypeStruct(sampled_t.shape, jnp.bfloat16),
            jax.ShapeDtypeStruct(projected.shape, F32),
        ),
        name="finish",
    )(sampled_t, projected)
    return sampled_t.T, projected.reshape(ops, rank, rank)


def solution(mesh):
    placed = (
        P(("sweep", "rows"), None),
        P(("sweep", "rows")),
        P(("sweep", "coef"), "rows", None, None, None),
        P(("sweep", "coef"), "rows"),
        P(("sweep", "coef"), "rows", None),
        P("sweep"),
    )
    return jax.shard_map(
        functools.partial(local, mesh.shape["rows"]),
        mesh=mesh,
        in_specs=placed,
        out_specs=(P(("sweep", "rows"), "coef"), P(("sweep", "coef"), None, None)),
        check_vma=False,
    )
```
